32 devices in a mesh: group: 4 (over z), dev: 8 (over y, x, core).
Axes of the slice: x: 2, y: 2, z: 4, core: 2. Of those that a mesh axis runs over, the one named last changes fastest.
Arguments:
- points: bfloat16 [131072, 64], P(('group', 'dev')), may hold values from -4 to 4
- weights: bfloat16 [131072, 64], P(('group', 'dev')), may hold values from -4 to 4
- near_leaves: int32 [256, 4], P(('group', 'dev')), may hold values from 0 to 63, as said below
- near_count: int32 [256], P(('group', 'dev')), may hold values from 1 to 4, as said below
- leaf_perm: int32 [256, 512], P(('group', 'dev')), may hold values from 0 to 511, each once within a row
- local_perm: int32 [32, 7, 512], P(('group', 'dev')), may hold values from 0 to 511, each once within a row
- upper_perm: int32 [30, 512], replicated, may hold values from 0 to 511, each once within a row
Outputs:
- product: float32 [131072, 64], P(('group', 'dev'))
The draws below stay inside these ranges and needn't reach their ends.
Inputs may be any that keep to these rules, and one draw needn't show every extreme that they name: `near_leaves`: leaf numbers count within the leaf's own group. Entry 0 is the leaf itself; entries 1 to near_count - 1 are distinct other leaves held by the same device or by the device just before or after it along dev in the same group; later entries repeat the leaf itself. `near_count`: at least one leaf of every group has exactly 4 live entries. `leaf_perm`: each row holds every number of 0 to 511 once. `local_perm`: each row holds every number of 0 to 511 once. `upper_perm`: each row holds every number of 0 to 511 once.
All inputs are finite; a program needn't handle non-finite values.
Results may differ from the reference program's by a relative error of at most 0.0062.
Values may be sent and summed in bfloat16 or wider, within the bound.
A program may use at most 64 MiB of HBM per device.

```python
import jax
import jax.numpy as jnp
from jax import lax

F = 64
R = 64
LEAF = 512
S = 256
NEAR_MOST = 4
LEAVES_DEV = 8
LEAVES_GROUP = 64
LEAVES = 256
POINTS = 131072
N_GROUP = 4
N_DEV = 8


def near_tables(key):
    key_load, key_count, key_peak, key_pick = jax.random.split(jax.random.fold_in(key, 11), 4)
    leaf_ids = jnp.arange(LEAVES, dtype=jnp.int32)
    device_loads = jnp.min(jax.random.randint(key_load, (3, LEAVES // LEAVES_DEV), 1, NEAR_MOST + 1), axis=0)
    raw_counts = jax.random.randint(key_count, (LEAVES,), 0, 1 << 20)
    near_counts = raw_counts % device_loads[leaf_ids // LEAVES_DEV] + 1
    in_group = leaf_ids % LEAVES_GROUP
    peak_leaf = jax.random.randint(key_peak, (LEAVES // LEAVES_GROUP,), 0, LEAVES_GROUP)
    near_counts = jnp.where(in_group == peak_leaf[leaf_ids // LEAVES_GROUP], NEAR_MOST, near_counts)
    window_span = 3 * LEAVES_DEV
    offsets = jnp.arange(window_span, dtype=jnp.int32)
    window_start = (in_group // LEAVES_DEV - 1) * LEAVES_DEV
    candidates = window_start[:, None] + offsets[None, :]
    usable = (candidates >= 0) & (candidates < LEAVES_GROUP) & (candidates != in_group[:, None])
    scores = jax.random.randint(key_pick, (LEAVES, window_span), 0, 1 << 16) * window_span + offsets[None, :]
    scores = scores + jnp.where(usable, 0, 1 << 24)
    picked = jnp.argsort(scores, axis=1)[:, :NEAR_MOST - 1]
    chosen = jnp.take_along_axis(candidates, picked, axis=1)
    near_lists = jnp.concatenate([in_group[:, None], chosen], axis=1)
    slot_ids = jnp.arange(NEAR_MOST, dtype=jnp.int32)
    near_lists = jnp.where(slot_ids[None, :] < near_counts[:, None], near_lists, in_group[:, None])
    return (near_lists.astype(jnp.int32), near_counts.astype(jnp.int32))


def draw_near_leaves(key, part):
    return near_tables(key)[0]


def draw_near_count(key, part):
    return near_tables(key)[1]


def draw_points(key, part):
    key = jax.random.fold_in(key, 3)
    feature_at = jnp.arange(F, dtype=jnp.float32)
    scales = jnp.exp(-2.302585 * feature_at / (F - 1))
    raw_values = jax.random.normal(key, (POINTS, F), jnp.float32)
    return jnp.clip(raw_values * scales[None, :], -4.0, 4.0).astype(jnp.bfloat16)


def level_of(stream_key, shape, cuts, smallest, high):
    factor_of = 1.0
    for axis_at, blocks in cuts:
        heights = jax.random.uniform(jax.random.fold_in(jax.random.fold_in(stream_key, 6), axis_at), (blocks,), jnp.float32, smallest / len(cuts), high / len(cuts))
        factor_of = factor_of * jnp.repeat(jnp.exp(heights), shape[axis_at] // blocks).reshape((-1,) + (1,) * (len(shape) - 1 - axis_at))
    return factor_of


def centred(rng, dims, scale, reach, cuts=(), kind=jnp.bfloat16):
    level = level_of(rng, dims, cuts, -0.22, 0.18) if cuts else 1.0
    values = jax.random.normal(rng, dims, jnp.float32) * scale * level
    return jnp.minimum(jnp.maximum(values, -reach), reach).astype(kind)


def setup_inputs(seed: int = 0) -> dict:
    key_list = jax.random.split(jax.random.key(seed), 8)
    points = draw_points(jax.random.fold_in(key_list[7], 71), 0)
    weights = centred(key_list[1], (POINTS, R), 1.0, 4.0, ((0, 32),))
    near_leaves = draw_near_leaves(jax.random.fold_in(key_list[7], 71), 0)
    near_count = draw_near_count(jax.random.fold_in(key_list[7], 71), 0)
    leaf_perm = jax.vmap(lambda own: jax.random.permutation(own, LEAF))(jax.random.split(key_list[4], LEAVES)).reshape((LEAVES, LEAF)).astype(jnp.int32)
    local_perm = jax.vmap(lambda own: jax.random.permutation(own, 2 * S))(jax.random.split(key_list[5], (N_DEV * N_GROUP) * (LEAVES_DEV - 1))).reshape((N_DEV * N_GROUP, LEAVES_DEV - 1, 2 * S)).astype(jnp.int32)
    upper_perm = jax.vmap(lambda own: jax.random.permutation(own, 2 * S))(jax.random.split(key_list[6], (N_DEV * N_GROUP - 2))).reshape((N_DEV * N_GROUP - 2, 2 * S)).astype(jnp.int32)
    return dict(points=points, weights=weights, near_leaves=near_leaves, near_count=near_count, leaf_perm=leaf_perm, local_perm=local_perm, upper_perm=upper_perm)


spread_width = 10.0
merge_gain = 0.8408964152537145


def kernel_block(left, right):
    left_sq = jnp.sum(jnp.square(left.astype(jnp.float32)), axis=-1)
    right_sq = jnp.sum(jnp.square(right.astype(jnp.float32)), axis=-1)
    cross = jnp.dot(left, right.T, preferred_element_type=jnp.float32)
    return jnp.exp(-(left_sq[:, None] + right_sq[None, :] - 2.0 * cross) / spread_width)


def merge_node(stacked, ordering, feat_cols):
    skel_rows = ordering.shape[0] // 2
    head_rows = stacked[ordering[:skel_rows]]
    tail_rows = stacked[ordering[skel_rows:]]
    summed = head_rows[:, feat_cols:].astype(jnp.float32) + tail_rows[:, feat_cols:].astype(jnp.float32)
    merged = (merge_gain * summed).astype(jnp.bfloat16)
    return jnp.concatenate([head_rows[:, :feat_cols], merged], axis=1)


def far_term(own_rows, sibling, feat_cols):
    block = kernel_block(own_rows[:, :feat_cols], sibling[:, :feat_cols]).astype(jnp.bfloat16)
    return jnp.dot(block, sibling[:, feat_cols:], preferred_element_type=jnp.float32)


def expand(values, ordering):
    skel_rows = ordering.shape[0] // 2
    spread = jnp.zeros((ordering.shape[0], values.shape[1]), jnp.float32)
    return spread.at[ordering[:skel_rows]].set(values).at[ordering[skel_rows:]].set(values)


def reference(points, weights, near_leaves, near_count, leaf_perm, local_perm, upper_perm):
    feat_cols = points.shape[1]
    rhs_cols = weights.shape[1]
    leaves_all, leaf_rows = leaf_perm.shape
    leaves_here = LEAVES_DEV
    per_group = LEAVES_GROUP
    stacked = jnp.concatenate([points, weights], axis=1)
    blocks = stacked.reshape(leaves_all, leaf_rows, feat_cols + rhs_cols)

    def near_leaf(leaf_args):
        leaf_index, own_block, live_count, near_row = leaf_args
        group_start = (leaf_index // per_group) * per_group

        def add_slot(slot_no, summed):
            sibling = lax.dynamic_index_in_dim(blocks, group_start + near_row[slot_no], 0, keepdims=False)
            block = kernel_block(own_block[:, :feat_cols], sibling[:, :feat_cols]).astype(jnp.bfloat16)
            term = jnp.dot(block, sibling[:, feat_cols:], preferred_element_type=jnp.float32)
            return summed + jnp.where(slot_no < live_count, term, jnp.zeros_like(term))

        return lax.fori_loop(0, near_row.shape[0], add_slot, jnp.zeros((leaf_rows, rhs_cols), jnp.float32))

    near_part = lax.map(near_leaf, (jnp.arange(leaves_all, dtype=jnp.int32), blocks, near_count, near_leaves))

    def merge_all(stacks, orderings):
        return jax.vmap(lambda one_stack, one_order: merge_node(one_stack, one_order, feat_cols))(stacks, orderings)

    def far_one(node_pair):
        return far_term(node_pair[0], node_pair[1], feat_cols)

    branches = merge_all(blocks, leaf_perm)
    tree_levels = leaves_all.bit_length() - 1
    local_levels = leaves_here.bit_length() - 1
    device_nodes = leaves_all // leaves_here
    far_list = []
    order_list = []
    for tree_level in range(tree_levels):
        node_count = branches.shape[0]
        partner = branches.reshape(node_count // 2, 2, branches.shape[1], branches.shape[2])[:, ::-1]
        partner = partner.reshape(branches.shape)
        far_list.append(lax.map(far_one, (branches, partner)))
        if tree_level + 1 < tree_levels:
            parent_level = tree_level + 1
            if parent_level <= local_levels:
                first_row = leaves_here - leaves_here // 2 ** (parent_level - 1)
                ordering = local_perm[:, first_row:first_row + leaves_here // 2 ** parent_level]
                ordering = ordering.reshape(-1, local_perm.shape[2])
            else:
                upper_bit = parent_level - local_levels - 1
                first_row = device_nodes - device_nodes // 2 ** upper_bit
                ordering = upper_perm[first_row:first_row + device_nodes // 2 ** (upper_bit + 1)]
            order_list.append(ordering)
            paired = branches.reshape(node_count // 2, 2 * branches.shape[1], branches.shape[2])
            branches = merge_all(paired, ordering)
    descent = far_list[-1]
    for tree_level in range(tree_levels - 2, -1, -1):
        spread = jax.vmap(expand)(descent, order_list[tree_level])
        descent = far_list[tree_level] + merge_gain * spread.reshape(far_list[tree_level].shape)
    result = near_part + merge_gain * jax.vmap(expand)(descent, leaf_perm)
    return result.reshape(-1, rhs_cols)
```

```python
import functools
import math

import jax
import jax.numpy as jnp
from jax import lax
from jax.experimental import pallas as pl
from jax.experimental.pallas import tpu as pltpu
from jax.sharding import PartitionSpec as P

spread_width = 10.0
merge_gain = 0.8408964152537145
exp2_scale = 2.0 / spread_width * math.log2(math.e)
bf16 = jnp.bfloat16
f32 = jnp.float32


def half_squares(coords):
    wide = coords.astype(f32)
    total = -0.5 * jnp.sum(wide * wide, axis=0, keepdims=True)
    high = total.astype(bf16).astype(f32)
    rest = total - high
    mid = rest.astype(bf16).astype(f32)
    return high, mid, rest - mid


def with_squares(coords, squares_first):
    high, mid, low = half_squares(coords)
    shape = (16, coords.shape[1])
    row = lax.broadcasted_iota(jnp.int32, shape, 0)
    at = 0 if squares_first else 3
    ones = (row >= 3 - at) & (row < 6 - at)
    extra = jnp.where(ones, 1.0, 0.0)
    for offset, part in enumerate((high, mid, low)):
        extra = jnp.where(row == at + offset, jnp.broadcast_to(part, shape), extra)
    return jnp.concatenate([coords, extra.astype(bf16)], axis=0)


def kernel_block(source, target):
    inner = lax.dot_general(source, target, (((0,), (0,)), ((), ())), preferred_element_type=f32)
    return jnp.exp2(inner * exp2_scale).astype(bf16)


def apply(rhs, block):
    return jnp.dot(rhs, block, preferred_element_type=f32)


def apply_flipped(rhs, block):
    return lax.dot_general(rhs, block, (((1,), (1,)), ((), ())), preferred_element_type=f32)


def tables(order, head_ref, both_ref, at):
    size = order.shape[1]
    half = size // 2
    row = lax.broadcasted_iota(jnp.int32, (size, half), 0)
    head = order[:, :half] == row
    tail = order[:, half:] == row
    head_ref[at] = jnp.where(head, 1.0, 0.0).astype(bf16)
    both_ref[at] = jnp.where(head | tail, 1.0, 0.0).astype(bf16)


def merge(coords, rhs, head, both):
    picked = jnp.dot(coords, head, preferred_element_type=f32).astype(bf16)
    summed = merge_gain * jnp.dot(rhs, both, preferred_element_type=f32)
    return jnp.concatenate([picked, summed.astype(bf16)], axis=0)


def expand(values, both):
    high = values.astype(bf16)
    low = (values - high.astype(f32)).astype(bf16)
    spread = apply_flipped(jnp.concatenate([high, low], axis=0), both)
    rows = values.shape[0]
    return spread[:rows] + spread[rows:]


def tree_kernel(
    leaves,
    leaf_rows,
    feat,
    dev_count,
    group_count,
    p_ref,
    w_ref,
    leaf_ref,
    local_ref,
    upper_ref,
    part_ref,
    winp_ref,
    winw_ref,
    stack,
    head_t,
    both_t,
    far,
    down,
    send_sem,
    recv_sem,
    halo_send,
    halo_recv,
    own_sem,
):
    skel = leaf_rows // 2
    devices = dev_count * group_count
    dev_bits = dev_count.bit_length() - 1
    group_bits = group_count.bit_length() - 1
    rounds = dev_bits + group_bits
    local_levels = leaves.bit_length() - 1
    dev = lax.axis_index("dev")
    group = lax.axis_index("group")
    flat = group * dev_count + dev

    def partner(height):
        if height < dev_bits:
            side = dev // 2**height % 2
            return {"dev": dev + (1 - 2 * side) * 2**height}, side
        stride = 2 ** (height - dev_bits)
        side = group // stride % 2
        return {"group": group + (1 - 2 * side) * stride}, side

    barrier = pltpu.get_barrier_semaphore()
    for height in range(rounds):
        pl.semaphore_signal(
            barrier, inc=1, device_id=partner(height)[0], device_id_type=pl.DeviceIdType.MESH
        )

    beside = dev + 2 * lax.rem(dev, 2) - 1
    has_beside = (beside >= 0) & (beside < dev_count)

    @pl.when(has_beside)
    def _():
        pl.semaphore_signal(
            barrier, inc=1, device_id={"dev": beside}, device_id_type=pl.DeviceIdType.MESH
        )

    pl.semaphore_wait(barrier, rounds + has_beside.astype(jnp.int32))

    def halo(to_right):
        other = lax.rem(dev + 1, dev_count) if to_right else lax.rem(dev + dev_count - 1, dev_count)
        slot = 0 if to_right else 2
        row = 1 if to_right else 0
        return [
            pltpu.make_async_remote_copy(
                src_ref=src,
                dst_ref=dst.at[slot],
                send_sem=halo_send.at[row, k],
                recv_sem=halo_recv.at[row, k],
                device_id={"dev": other},
                device_id_type=pl.DeviceIdType.MESH,
            )
            for k, (src, dst) in enumerate(((p_ref, winp_ref), (w_ref, winw_ref)))
        ]

    def start(copies):
        for copy in copies:
            copy.start()

    pl.when(dev > 0)(lambda: start(halo(False)))
    pl.when(dev < dev_count - 1)(lambda: start(halo(True)))
    own_copies = [
        pltpu.make_async_copy(p_ref, winp_ref.at[1], own_sem.at[0]),
        pltpu.make_async_copy(w_ref, winw_ref.at[1], own_sem.at[1]),
    ]
    start(own_copies)

    def leaf_cols(leaf):
        return pl.ds(pl.multiple_of(leaf * leaf_rows, leaf_rows), leaf_rows)

    pair_base = [leaves - leaves // 2**t for t in range(local_levels)]
    top_pair = leaves - 1
    node_base = [2 * base for base in pair_base]
    top_node = 2 * top_pair
    table_base = [0] + [leaves + base for base in pair_base]
    top_table = 2 * leaves - 1

    def up_leaves(pair, carry):
        for k in range(2):
            leaf = 2 * pair + k
            tables(leaf_ref[pl.ds(leaf, 1), :], head_t, both_t, leaf)
            cols = leaf_cols(leaf)
            stack[pair, k] = merge(p_ref[:, cols], w_ref[:, cols], head_t[leaf], both_t[leaf])
        return carry

    lax.fori_loop(0, leaves // 2, up_leaves, 0)

    def merge_pair(pair, table):
        two = jnp.concatenate([stack[pair, 0], stack[pair, 1]], axis=1)
        return merge(two[:feat], two[feat:], head_t[table], both_t[table])

    side0 = partner(0)[1]
    for t in range(local_levels):
        count = leaves // 2 ** (t + 1)
        for i in range(count):
            row = pair_base[t] + i
            tables(local_ref[row : row + 1, :], head_t, both_t, table_base[t + 1] + i)
            merged = merge_pair(pair_base[t] + i, table_base[t + 1] + i)
            if t + 1 < local_levels:
                stack[pair_base[t + 1] + i // 2, i % 2] = merged
            else:
                stack[top_pair, side0] = merged

    def local_far(pair, carry):
        first, second = stack[pair, 0], stack[pair, 1]
        block = kernel_block(with_squares(first[:feat], True), with_squares(second[:feat], False))
        far[2 * pair + 1] = apply(first[feat:], block)
        far[2 * pair] = apply_flipped(second[feat:], block)
        return carry

    def near_own(leaf, carry):
        cols = leaf_cols(leaf)
        coords = p_ref[:, cols]
        block = kernel_block(with_squares(coords, True), with_squares(coords, False))
        part_ref[:, cols] = apply(w_ref[:, cols], block)
        return carry

    def cross_far(height):
        side = partner(height)[1]
        own = stack[top_pair + height, side]
        other = stack[top_pair + height, 1 - side]
        block = kernel_block(with_squares(other[:feat], True), with_squares(own[:feat], False))
        far[top_node + height] = apply(other[feat:], block)

    def exchange(height):
        target, side = partner(height)
        return pltpu.make_async_remote_copy(
            src_ref=stack.at[top_pair + height, side],
            dst_ref=stack.at[top_pair + height, side],
            send_sem=send_sem.at[height],
            recv_sem=recv_sem.at[height],
            device_id=target,
            device_id_type=pl.DeviceIdType.MESH,
        )

    shares = max(rounds - 1, 1)
    bounds = [leaves * k // shares for k in range(shares + 1)]
    copies = []
    for height in range(rounds):
        copy = exchange(height)
        copy.start()
        copies.append(copy)
        if height == 0:
            for level in range(rounds - 1):
                row = devices - devices // 2**level + flat // 2 ** (level + 1)
                tables(upper_ref[pl.ds(row, 1), :], head_t, both_t, top_table + level)
            lax.fori_loop(0, leaves - 1, local_far, 0)
        else:
            cross_far(height - 1)
            if bounds[height] > bounds[height - 1]:
                lax.fori_loop(bounds[height - 1], bounds[height], near_own, 0)
        copy.wait_recv()
        if height + 1 < rounds:
            stack[top_pair + height + 1, partner(height + 1)[1]] = merge_pair(
                top_pair + height, top_table + height
            )
    cross_far(rounds - 1)
    if rounds == 1:
        lax.fori_loop(0, leaves, near_own, 0)

    descent = far[top_node + rounds - 1]
    for height in range(rounds - 2, -1, -1):
        rows = pl.ds(pl.multiple_of(partner(height + 0)[1] * skel, skel), skel)
        spread = expand(descent, both_t[top_table + height, rows, :])
        descent = far[top_node + height] + merge_gain * spread
    down[0] = descent
    for t in range(local_levels - 1, -1, -1):
        count = leaves // 2 ** (t + 1)
        values = [down[i] for i in range(count)]
        for i in range(count):
            spread = expand(values[i], both_t[table_base[t + 1] + i])
            node = node_base[t] + 2 * i
            down[2 * i] = far[node] + merge_gain * spread[:, :skel]
            down[2 * i + 1] = far[node + 1] + merge_gain * spread[:, skel:]

    def last(pair, carry):
        for k in range(2):
            leaf = 2 * pair + k
            part_ref[:, leaf_cols(leaf)] += merge_gain * expand(down[leaf], both_t[leaf])
        return carry

    lax.fori_loop(0, leaves // 2, last, 0)

    for copy in copies:
        copy.wait_send()

    def finish(sent, received):
        for copy in sent:
            copy.wait_send()
        for copy in received:
            copy.wait_recv()

    pl.when(dev > 0)(lambda: finish(halo(False), halo(True)))
    pl.when(dev < dev_count - 1)(lambda: finish(halo(True), halo(False)))
    for copy in own_copies:
        copy.wait()


def near_kernel(leaves, leaf_rows, near_ref, count_ref, part_ref, winp_ref, winw_ref, out_ref):
    first_leaf = (lax.axis_index("dev") - 1) * leaves

    def one_leaf(leaf, carry):
        cols = pl.ds(pl.multiple_of(leaf * leaf_rows, leaf_rows), leaf_rows)
        out_ref[:, cols] = part_ref[:, cols]
        target = with_squares(winp_ref[1, :, cols], False)

        def one_slot(slot, inner):
            place = near_ref[leaf, slot] - first_leaf
            side = place // leaves
            other = pl.ds(pl.multiple_of((place - side * leaves) * leaf_rows, leaf_rows), leaf_rows)
            block = kernel_block(with_squares(winp_ref[side, :, other], True), target)
            out_ref[:, cols] += apply(winw_ref[side, :, other], block)
            return inner

        lax.fori_loop(1, count_ref[leaf], one_slot, 0)
        return carry

    lax.fori_loop(0, leaves, one_leaf, 0)


def per_device(
    dev_count, group_count, points, weights, near_leaves, near_count, leaf_perm, local_perm, upper_perm
):
    feat = points.shape[1]
    rhs = weights.shape[1]
    rows = points.shape[0]
    leaves, leaf_rows = leaf_perm.shape
    skel = leaf_rows // 2
    rounds = (dev_count * group_count).bit_length() - 1
    vmem = pl.BlockSpec(memory_space=pltpu.VMEM)
    smem = pl.BlockSpec(memory_space=pltpu.SMEM)
    hbm = pl.BlockSpec(memory_space=pl.ANY)
    part, win_p, win_w = pl.pallas_call(
        functools.partial(tree_kernel, leaves, leaf_rows, feat, dev_count, group_count),
        out_shape=[
            jax.ShapeDtypeStruct((rhs, rows), f32),
            jax.ShapeDtypeStruct((3, feat, rows), bf16),
            jax.ShapeDtypeStruct((3, rhs, rows), bf16),
        ],
        in_specs=[vmem] * 5,
        out_specs=[vmem, hbm, hbm],
        scratch_shapes=[
            pltpu.VMEM((leaves - 1 + rounds, 2, feat + rhs, skel), bf16),
            pltpu.VMEM((2 * leaves - 2 + rounds, leaf_rows, skel), bf16),
            pltpu.VMEM((2 * leaves - 2 + rounds, leaf_rows, skel), bf16),
            pltpu.VMEM((2 * leaves - 2 + rounds, rhs, skel), f32),
            pltpu.VMEM((leaves, rhs, skel), f32),
            pltpu.SemaphoreType.DMA((rounds,)),
            pltpu.SemaphoreType.DMA((rounds,)),
            pltpu.SemaphoreType.DMA((2, 2)),
            pltpu.SemaphoreType.DMA((2, 2)),
            pltpu.SemaphoreType.DMA((2,)),
        ],
        compiler_params=pltpu.CompilerParams(
            collective_id=0, has_side_effects=True, vmem_limit_bytes=48 * 2**20
        ),
        name="tree",
    )(points.T, weights.T, leaf_perm, local_perm[0], upper_perm)
    product = pl.pallas_call(
        functools.partial(near_kernel, leaves, leaf_rows),
        out_shape=jax.ShapeDtypeStruct((rhs, rows), f32),
        in_specs=[smem, smem, vmem, vmem, vmem],
        out_specs=vmem,
        compiler_params=pltpu.CompilerParams(vmem_limit_bytes=48 * 2**20),
        name="near",
    )(near_leaves, near_count, part, win_p, win_w)
    return product.T


def solution(mesh):
    sizes = dict(mesh.shape)
    both = ("group", "dev")
    in_specs = (
        P(both, None),
        P(both, None),
        P(both, None),
        P(both),
        P(both, None),
        P(both, None, None),
        P(),
    )
    return jax.shard_map(
        functools.partial(per_device, sizes["dev"], sizes["group"]),
        mesh=mesh,
        in_specs=in_specs,
        out_specs=P(both, None),
        check_vma=False,
    )
```

```python
import functools
import math

import jax
import jax.numpy as jnp
from jax import lax
from jax.experimental import pallas as pl
from jax.experimental.pallas import tpu as pltpu
from jax.sharding import PartitionSpec as P

spread_width = 10.0
merge_gain = 0.8408964152537145
exp2_scale = 2.0 / spread_width * math.log2(math.e)
bf16 = jnp.bfloat16
f32 = jnp.float32


def half_squares(coords):
    wide = coords.astype(f32)
    total = -0.5 * jnp.sum(wide * wide, axis=0, keepdims=True)
    high = total.astype(bf16).astype(f32)
    rest = total - high
    mid = rest.astype(bf16).astype(f32)
    return high, mid, rest - mid


def with_squares(coords, squares_first):
    high, mid, low = half_squares(coords)
    shape = (16, coords.shape[1])
    row = lax.broadcasted_iota(jnp.int32, shape, 0)
    at = 0 if squares_first else 3
    ones = (row >= 3 - at) & (row < 6 - at)
    extra = jnp.where(ones, 1.0, 0.0)
    for offset, part in enumerate((high, mid, low)):
        extra = jnp.where(row == at + offset, jnp.broadcast_to(part, shape), extra)
    return jnp.concatenate([coords, extra.astype(bf16)], axis=0)


def kernel_block(source, target):
    inner = lax.dot_general(source, target, (((0,), (0,)), ((), ())), preferred_element_type=f32)
    return jnp.exp2(inner * exp2_scale).astype(bf16)


def apply(rhs, block):
    return jnp.dot(rhs, block, preferred_element_type=f32)


def apply_flipped(rhs, block):
    return lax.dot_general(rhs, block, (((1,), (1,)), ((), ())), preferred_element_type=f32)


def tables(order, head_ref, both_ref, at):
    size = order.shape[1]
    half = size // 2
    row = lax.broadcasted_iota(jnp.int32, (size, half), 0)
    head = order[:, :half] == row
    tail = order[:, half:] == row
    head_ref[at] = jnp.where(head, 1.0, 0.0).astype(bf16)
    both_ref[at] = jnp.where(head | tail, 1.0, 0.0).astype(bf16)


def merge(coords, rhs, head, both):
    picked = jnp.dot(coords, head, preferred_element_type=f32).astype(bf16)
    summed = merge_gain * jnp.dot(rhs, both, preferred_element_type=f32)
    return jnp.concatenate([picked, summed.astype(bf16)], axis=0)


def expand(values, both):
    high = values.astype(bf16)
    low = (values - high.astype(f32)).astype(bf16)
    spread = apply_flipped(jnp.concatenate([high, low], axis=0), both)
    rows = values.shape[0]
    return spread[:rows] + spread[rows:]


def tree_kernel(
    leaves,
    leaf_rows,
    feat,
    dev_count,
    group_count,
    p_hbm,
    w_hbm,
    leaf_hbm,
    local_hbm,
    upper_hbm,
    part_ref,
    winp_ref,
    winw_ref,
    stack,
    head_t,
    both_t,
    far,
    down,
    send_sem,
    recv_sem,
    halo_send,
    halo_recv,
    own_sem,
    p_ref,
    w_ref,
    leaf_ref,
    local_ref,
    upper_ref,
    load_sem,
):
    skel = leaf_rows // 2
    devices = dev_count * group_count
    dev_bits = dev_count.bit_length() - 1
    group_bits = group_count.bit_length() - 1
    rounds = dev_bits + group_bits
    local_levels = leaves.bit_length() - 1
    dev = lax.axis_index("dev")
    group = lax.axis_index("group")
    flat = group * dev_count + dev

    def partner(height):
        if height < dev_bits:
            side = dev // 2**height % 2
            return {"dev": dev + (1 - 2 * side) * 2**height}, side
        stride = 2 ** (height - dev_bits)
        side = group // stride % 2
        return {"group": group + (1 - 2 * side) * stride}, side

    loads = [
        pltpu.make_async_copy(src, dst, load_sem.at[k])
        for k, (src, dst) in enumerate(
            (
                (leaf_hbm, leaf_ref),
                (p_hbm, p_ref),
                (w_hbm, w_ref),
                (local_hbm, local_ref),
                (upper_hbm, upper_ref),
            )
        )
    ]
    for load in loads:
        load.start()
    barrier = pltpu.get_barrier_semaphore()
    for height in range(rounds):
        pl.semaphore_signal(
            barrier, inc=1, device_id=partner(height)[0], device_id_type=pl.DeviceIdType.MESH
        )

    beside = dev + 2 * lax.rem(dev, 2) - 1
    has_beside = (beside >= 0) & (beside < dev_count)

    @pl.when(has_beside)
    def _():
        pl.semaphore_signal(
            barrier, inc=1, device_id={"dev": beside}, device_id_type=pl.DeviceIdType.MESH
        )

    pl.semaphore_wait(barrier, rounds + has_beside.astype(jnp.int32))

    def halo(to_right):
        other = lax.rem(dev + 1, dev_count) if to_right else lax.rem(dev + dev_count - 1, dev_count)
        slot = 0 if to_right else 2
        row = 1 if to_right else 0
        return [
            pltpu.make_async_remote_copy(
                src_ref=src,
                dst_ref=dst.at[slot],
                send_sem=halo_send.at[row, k],
                recv_sem=halo_recv.at[row, k],
                device_id={"dev": other},
                device_id_type=pl.DeviceIdType.MESH,
            )
            for k, (src, dst) in enumerate(((p_hbm, winp_ref), (w_hbm, winw_ref)))
        ]

    def start(copies):
        for copy in copies:
            copy.start()

    pl.when(dev > 0)(lambda: start(halo(False)))
    pl.when(dev < dev_count - 1)(lambda: start(halo(True)))
    own_copies = [
        pltpu.make_async_copy(p_hbm, winp_ref.at[1], own_sem.at[0]),
        pltpu.make_async_copy(w_hbm, winw_ref.at[1], own_sem.at[1]),
    ]
    start(own_copies)
    for load in loads:
        load.wait()

    def leaf_cols(leaf):
        return pl.ds(pl.multiple_of(leaf * leaf_rows, leaf_rows), leaf_rows)

    pair_base = [leaves - leaves // 2**t for t in range(local_levels)]
    top_pair = leaves - 1
    node_base = [2 * base for base in pair_base]
    top_node = 2 * top_pair
    table_base = [0] + [leaves + base for base in pair_base]
    top_table = 2 * leaves - 1

    def up_leaves(pair, carry):
        for k in range(2):
            leaf = 2 * pair + k
            tables(leaf_ref[pl.ds(leaf, 1), :], head_t, both_t, leaf)
            cols = leaf_cols(leaf)
            stack[pair, k] = merge(p_ref[:, cols], w_ref[:, cols], head_t[leaf], both_t[leaf])
        return carry

    lax.fori_loop(0, leaves // 2, up_leaves, 0)

    def merge_pair(pair, table):
        two = jnp.concatenate([stack[pair, 0], stack[pair, 1]], axis=1)
        return merge(two[:feat], two[feat:], head_t[table], both_t[table])

    side0 = partner(0)[1]
    for t in range(local_levels):
        count = leaves // 2 ** (t + 1)
        for i in range(count):
            row = pair_base[t] + i
            tables(local_ref[row], head_t, both_t, table_base[t + 1] + i)
            merged = merge_pair(pair_base[t] + i, table_base[t + 1] + i)
            if t + 1 < local_levels:
                stack[pair_base[t + 1] + i // 2, i % 2] = merged
            else:
                stack[top_pair, side0] = merged

    def local_far(pair, carry):
        first, second = stack[pair, 0], stack[pair, 1]
        block = kernel_block(with_squares(first[:feat], True), with_squares(second[:feat], False))
        far[2 * pair + 1] = apply(first[feat:], block)
        far[2 * pair] = apply_flipped(second[feat:], block)
        return carry

    def near_own(leaf, carry):
        cols = leaf_cols(leaf)
        coords = p_ref[:, cols]
        block = kernel_block(with_squares(coords, True), with_squares(coords, False))
        part_ref[:, cols] = apply(w_ref[:, cols], block)
        return carry

    def cross_far(height):
        side = partner(height)[1]
        own = stack[top_pair + height, side]
        other = stack[top_pair + height, 1 - side]
        block = kernel_block(with_squares(other[:feat], True), with_squares(own[:feat], False))
        far[top_node + height] = apply(other[feat:], block)

    def exchange(height):
        target, side = partner(height)
        return pltpu.make_async_remote_copy(
            src_ref=stack.at[top_pair + height, side],
            dst_ref=stack.at[top_pair + height, side],
            send_sem=send_sem.at[height],
            recv_sem=recv_sem.at[height],
            device_id=target,
            device_id_type=pl.DeviceIdType.MESH,
        )

    shares = max(rounds - 1, 1)
    bounds = [leaves * k // shares for k in range(shares + 1)]
    far_bounds = [(leaves - 1) * k // shares for k in range(shares + 1)]
    copies = []
    for height in range(rounds):
        copy = exchange(height)
        copy.start()
        copies.append(copy)
        if height == 0:
            for level in range(rounds - 1):
                row = devices - devices // 2**level + flat // 2 ** (level + 1)
                tables(upper_ref[pl.ds(row, 1), :], head_t, both_t, top_table + level)
        else:
            cross_far(height - 1)
            if bounds[height] > bounds[height - 1]:
                lax.fori_loop(bounds[height - 1], bounds[height], near_own, 0)
            if far_bounds[height] > far_bounds[height - 1]:
                lax.fori_loop(far_bounds[height - 1], far_bounds[height], local_far, 0)
        copy.wait_recv()
        if height + 1 < rounds:
            stack[top_pair + height + 1, partner(height + 1)[1]] = merge_pair(
                top_pair + height, top_table + height
            )
    cross_far(rounds - 1)
    if rounds == 1:
        lax.fori_loop(0, leaves, near_own, 0)
        lax.fori_loop(0, leaves - 1, local_far, 0)

    descent = far[top_node + rounds - 1]
    for height in range(rounds - 2, -1, -1):
        rows = pl.ds(pl.multiple_of(partner(height + 0)[1] * skel, skel), skel)
        spread = expand(descent, both_t[top_table + height, rows, :])
        descent = far[top_node + height] + merge_gain * spread
    down[0] = descent
    for t in range(local_levels - 1, -1, -1):
        count = leaves // 2 ** (t + 1)
        values = [down[i] for i in range(count)]
        for i in range(count):
            spread = expand(values[i], both_t[table_base[t + 1] + i])
            node = node_base[t] + 2 * i
            down[2 * i] = far[node] + merge_gain * spread[:, :skel]
            down[2 * i + 1] = far[node + 1] + merge_gain * spread[:, skel:]

    def last(pair, carry):
        for k in range(2):
            leaf = 2 * pair + k
            part_ref[:, leaf_cols(leaf)] += merge_gain * expand(down[leaf], both_t[leaf])
        return carry

    lax.fori_loop(0, leaves // 2, last, 0)

    for copy in copies:
        copy.wait_send()

    def finish(sent, received):
        for copy in sent:
            copy.wait_send()
        for copy in received:
            copy.wait_recv()

    pl.when(dev > 0)(lambda: finish(halo(False), halo(True)))
    pl.when(dev < dev_count - 1)(lambda: finish(halo(True), halo(False)))
    for copy in own_copies:
        copy.wait()


def near_kernel(leaves, leaf_rows, near_ref, count_ref, part_ref, winp_ref, winw_ref, out_ref):
    first_leaf = (lax.axis_index("dev") - 1) * leaves

    def one_leaf(leaf, carry):
        cols = pl.ds(pl.multiple_of(leaf * leaf_rows, leaf_rows), leaf_rows)
        out_ref[:, cols] = part_ref[:, cols]
        target = with_squares(winp_ref[1, :, cols], False)

        def one_slot(slot, inner):
            place = near_ref[slot, leaf] - first_leaf
            side = place // leaves
            other = pl.ds(pl.multiple_of((place - side * leaves) * leaf_rows, leaf_rows), leaf_rows)
            block = kernel_block(with_squares(winp_ref[side, :, other], True), target)
            out_ref[:, cols] += apply(winw_ref[side, :, other], block)
            return inner

        lax.fori_loop(1, count_ref[leaf], one_slot, 0)
        return carry

    lax.fori_loop(0, leaves, one_leaf, 0)


def per_device(
    dev_count, group_count, points, weights, near_leaves, near_count, leaf_perm, local_perm, upper_perm
):
    feat = points.shape[1]
    rhs = weights.shape[1]
    rows = points.shape[0]
    leaves, leaf_rows = leaf_perm.shape
    skel = leaf_rows // 2
    rounds = (dev_count * group_count).bit_length() - 1
    vmem = pl.BlockSpec(memory_space=pltpu.VMEM)
    smem = pl.BlockSpec(memory_space=pltpu.SMEM)
    hbm = pl.BlockSpec(memory_space=pltpu.HBM)
    part, win_p, win_w = pl.pallas_call(
        functools.partial(tree_kernel, leaves, leaf_rows, feat, dev_count, group_count),
        out_shape=[
            jax.ShapeDtypeStruct((rhs, rows), f32),
            jax.ShapeDtypeStruct((3, feat, rows), bf16),
            jax.ShapeDtypeStruct((3, rhs, rows), bf16),
        ],
        in_specs=[hbm] * 5,
        out_specs=[vmem, hbm, hbm],
        scratch_shapes=[
            pltpu.VMEM((leaves - 1 + rounds, 2, feat + rhs, skel), bf16),
            pltpu.VMEM((2 * leaves - 2 + rounds, leaf_rows, skel), bf16),
            pltpu.VMEM((2 * leaves - 2 + rounds, leaf_rows, skel), bf16),
            pltpu.VMEM((2 * leaves - 2 + rounds, rhs, skel), f32),
            pltpu.VMEM((leaves, rhs, skel), f32),
            pltpu.SemaphoreType.DMA((rounds,)),
            pltpu.SemaphoreType.DMA((rounds,)),
            pltpu.SemaphoreType.DMA((2, 2)),
            pltpu.SemaphoreType.DMA((2, 2)),
            pltpu.SemaphoreType.DMA((2,)),
            pltpu.VMEM((feat, rows), bf16),
            pltpu.VMEM((rhs, rows), bf16),
            pltpu.VMEM(leaf_perm.shape, jnp.int32),
            pltpu.VMEM((leaves - 1, 1, leaf_rows), jnp.int32),
            pltpu.VMEM(upper_perm.shape, jnp.int32),
            pltpu.SemaphoreType.DMA((5,)),
        ],
        compiler_params=pltpu.CompilerParams(
            collective_id=0, has_side_effects=True, vmem_limit_bytes=48 * 2**20
        ),
        name="tree",
    )(points.T, weights.T, leaf_perm, jnp.transpose(local_perm, (1, 0, 2)), upper_perm)
    product = pl.pallas_call(
        functools.partial(near_kernel, leaves, leaf_rows),
        out_shape=jax.ShapeDtypeStruct((rhs, rows), f32),
        in_specs=[smem, smem, vmem, vmem, vmem],
        out_specs=vmem,
        compiler_params=pltpu.CompilerParams(vmem_limit_bytes=48 * 2**20),
        name="near",
    )(near_leaves.T, near_count, part, win_p, win_w)
    return product.T


def solution(mesh):
    sizes = dict(mesh.shape)
    both = ("group", "dev")
    in_specs = (
        P(both, None),
        P(both, None),
        P(both, None),
        P(both),
        P(both, None),
        P(both, None, None),
        P(),
    )
    return jax.shard_map(
        functools.partial(per_device, sizes["dev"], sizes["group"]),
        mesh=mesh,
        in_specs=in_specs,
        out_specs=P(both, None),
        check_vma=False,
    )
```

```python
import functools
import math

import jax
import jax.numpy as jnp
from jax import lax
from jax.experimental import pallas as pl
from jax.experimental.pallas import tpu as pltpu
from jax.sharding import PartitionSpec as P

spread_width = 10.0
merge_gain = 0.8408964152537145
exp2_scale = 2.0 / spread_width * math.log2(math.e)
bf16 = jnp.bfloat16
f32 = jnp.float32


def half_squares(coords):
    wide = coords.astype(f32)
    total = -0.5 * jnp.sum(wide * wide, axis=0, keepdims=True)
    high = total.astype(bf16).astype(f32)
    rest = total - high
    mid = rest.astype(bf16).astype(f32)
    return high, mid, rest - mid


def with_squares(coords, squares_first):
    high, mid, low = half_squares(coords)
    shape = (16, coords.shape[1])
    row = lax.broadcasted_iota(jnp.int32, shape, 0)
    at = 0 if squares_first else 3
    ones = (row >= 3 - at) & (row < 6 - at)
    extra = jnp.where(ones, 1.0, 0.0)
    for offset, part in enumerate((high, mid, low)):
        extra = jnp.where(row == at + offset, jnp.broadcast_to(part, shape), extra)
    return jnp.concatenate([coords, extra.astype(bf16)], axis=0)


def kernel_block(source, target):
    inner = lax.dot_general(source, target, (((0,), (0,)), ((), ())), preferred_element_type=f32)
    return jnp.exp2(inner * exp2_scale).astype(bf16)


def apply(rhs, block):
    return jnp.dot(rhs, block, preferred_element_type=f32)


def apply_flipped(rhs, block):
    return lax.dot_general(rhs, block, (((1,), (1,)), ((), ())), preferred_element_type=f32)


def tables(order, head_ref, both_ref, at):
    size = order.shape[1]
    half = size // 2
    row = lax.broadcasted_iota(jnp.int32, (size, half), 0)
    head = order[:, :half] == row
    tail = order[:, half:] == row
    head_ref[at] = jnp.where(head, 1.0, 0.0).astype(bf16)
    both_ref[at] = jnp.where(head | tail, 1.0, 0.0).astype(bf16)


def merge(coords, rhs, head, both):
    picked = jnp.dot(coords, head, preferred_element_type=f32).astype(bf16)
    summed = merge_gain * jnp.dot(rhs, both, preferred_element_type=f32)
    return jnp.concatenate([picked, summed.astype(bf16)], axis=0)


def expand(values, both):
    high = values.astype(bf16)
    low = (values - high.astype(f32)).astype(bf16)
    spread = apply_flipped(jnp.concatenate([high, low], axis=0), both)
    rows = values.shape[0]
    return spread[:rows] + spread[rows:]


def tree_kernel(
    leaves,
    leaf_rows,
    feat,
    dev_count,
    group_count,
    p_hbm,
    w_hbm,
    leaf_hbm,
    local_hbm,
    upper_hbm,
    part_ref,
    winp_ref,
    winw_ref,
    stack,
    head_t,
    both_t,
    far,
    down,
    send_sem,
    recv_sem,
    halo_send,
    halo_recv,
    p_ref,
    w_ref,
    leaf_ref,
    local_ref,
    upper_ref,
    load_sem,
):
    skel = leaf_rows // 2
    devices = dev_count * group_count
    dev_bits = dev_count.bit_length() - 1
    group_bits = group_count.bit_length() - 1
    rounds = dev_bits + group_bits
    local_levels = leaves.bit_length() - 1
    dev = lax.axis_index("dev")
    group = lax.axis_index("group")
    flat = group * dev_count + dev

    def partner(height):
        if height < dev_bits:
            side = dev // 2**height % 2
            return {"dev": dev + (1 - 2 * side) * 2**height}, side
        stride = 2 ** (height - dev_bits)
        side = group // stride % 2
        return {"group": group + (1 - 2 * side) * stride}, side

    loads = [
        pltpu.make_async_copy(src, dst, load_sem.at[k])
        for k, (src, dst) in enumerate(
            (
                (leaf_hbm, leaf_ref),
                (p_hbm, p_ref),
                (w_hbm, w_ref),
                (local_hbm, local_ref),
                (upper_hbm, upper_ref),
            )
        )
    ]
    for load in loads:
        load.start()
    barrier = pltpu.get_barrier_semaphore()
    for height in range(rounds):
        pl.semaphore_signal(
            barrier, inc=1, device_id=partner(height)[0], device_id_type=pl.DeviceIdType.MESH
        )

    beside = dev + 2 * lax.rem(dev, 2) - 1
    has_beside = (beside >= 0) & (beside < dev_count)

    @pl.when(has_beside)
    def _():
        pl.semaphore_signal(
            barrier, inc=1, device_id={"dev": beside}, device_id_type=pl.DeviceIdType.MESH
        )

    pl.semaphore_wait(barrier, rounds + has_beside.astype(jnp.int32))

    def halo(to_right):
        other = lax.rem(dev + 1, dev_count) if to_right else lax.rem(dev + dev_count - 1, dev_count)
        slot = 0 if to_right else 1
        row = 1 if to_right else 0
        return [
            pltpu.make_async_remote_copy(
                src_ref=src,
                dst_ref=dst.at[slot],
                send_sem=halo_send.at[row, k],
                recv_sem=halo_recv.at[row, k],
                device_id={"dev": other},
                device_id_type=pl.DeviceIdType.MESH,
            )
            for k, (src, dst) in enumerate(((p_hbm, winp_ref), (w_hbm, winw_ref)))
        ]

    def start(copies):
        for copy in copies:
            copy.start()

    pl.when(dev > 0)(lambda: start(halo(False)[:1]))
    pl.when(dev < dev_count - 1)(lambda: start(halo(True)[:1]))
    for load in loads:
        load.wait()

    def leaf_cols(leaf):
        return pl.ds(pl.multiple_of(leaf * leaf_rows, leaf_rows), leaf_rows)

    pair_base = [leaves - leaves // 2**t for t in range(local_levels)]
    top_pair = leaves - 1
    node_base = [2 * base for base in pair_base]
    top_node = 2 * top_pair
    table_base = [0] + [leaves + base for base in pair_base]
    top_table = 2 * leaves - 1

    def up_leaves(pair, carry):
        for k in range(2):
            leaf = 2 * pair + k
            tables(leaf_ref[pl.ds(leaf, 1), :], head_t, both_t, leaf)
            cols = leaf_cols(leaf)
            stack[pair, k] = merge(p_ref[:, cols], w_ref[:, cols], head_t[leaf], both_t[leaf])
        return carry

    lax.fori_loop(0, leaves // 2, up_leaves, 0)

    def merge_pair(pair, table):
        two = jnp.concatenate([stack[pair, 0], stack[pair, 1]], axis=1)
        return merge(two[:feat], two[feat:], head_t[table], both_t[table])

    side0 = partner(0)[1]
    for t in range(local_levels):
        count = leaves // 2 ** (t + 1)
        for i in range(count):
            row = pair_base[t] + i
            tables(local_ref[row], head_t, both_t, table_base[t + 1] + i)
            merged = merge_pair(pair_base[t] + i, table_base[t + 1] + i)
            if t + 1 < local_levels:
                stack[pair_base[t + 1] + i // 2, i % 2] = merged
            else:
                stack[top_pair, side0] = merged

    def local_far(pair, carry):
        first, second = stack[pair, 0], stack[pair, 1]
        block = kernel_block(with_squares(first[:feat], True), with_squares(second[:feat], False))
        far[2 * pair + 1] = apply(first[feat:], block)
        far[2 * pair] = apply_flipped(second[feat:], block)
        return carry

    def near_own(leaf, carry):
        cols = leaf_cols(leaf)
        coords = p_ref[:, cols]
        block = kernel_block(with_squares(coords, True), with_squares(coords, False))
        part_ref[:, cols] = apply(w_ref[:, cols], block)
        return carry

    def cross_far(height):
        side = partner(height)[1]
        own = stack[top_pair + height, side]
        other = stack[top_pair + height, 1 - side]
        block = kernel_block(with_squares(other[:feat], True), with_squares(own[:feat], False))
        far[top_node + height] = apply(other[feat:], block)

    def exchange(height):
        target, side = partner(height)
        return pltpu.make_async_remote_copy(
            src_ref=stack.at[top_pair + height, side],
            dst_ref=stack.at[top_pair + height, side],
            send_sem=send_sem.at[height],
            recv_sem=recv_sem.at[height],
            device_id=target,
            device_id_type=pl.DeviceIdType.MESH,
        )

    shares = max(rounds - 1, 1)
    bounds = [leaves * k // shares for k in range(shares + 1)]
    far_bounds = [(leaves - 1) * k // shares for k in range(shares + 1)]
    copies = []
    for height in range(rounds):
        copy = exchange(height)
        copy.start()
        copies.append(copy)
        if height == 0:
            for level in range(rounds - 1):
                row = devices - devices // 2**level + flat // 2 ** (level + 1)
                tables(upper_ref[pl.ds(row, 1), :], head_t, both_t, top_table + level)
        else:
            cross_far(height - 1)
            if bounds[height] > bounds[height - 1]:
                lax.fori_loop(bounds[height - 1], bounds[height], near_own, 0)
            if far_bounds[height] > far_bounds[height - 1]:
                lax.fori_loop(far_bounds[height - 1], far_bounds[height], local_far, 0)
        copy.wait_recv()
        if height == min(1, rounds - 1):
            pl.when(dev > 0)(lambda: start(halo(False)[1:]))
            pl.when(dev < dev_count - 1)(lambda: start(halo(True)[1:]))
        if height + 1 < rounds:
            stack[top_pair + height + 1, partner(height + 1)[1]] = merge_pair(
                top_pair + height, top_table + height
            )
    cross_far(rounds - 1)
    if rounds == 1:
        lax.fori_loop(0, leaves, near_own, 0)
        lax.fori_loop(0, leaves - 1, local_far, 0)

    descent = far[top_node + rounds - 1]
    for height in range(rounds - 2, -1, -1):
        rows = pl.ds(pl.multiple_of(partner(height + 0)[1] * skel, skel), skel)
        spread = expand(descent, both_t[top_table + height, rows, :])
        descent = far[top_node + height] + merge_gain * spread
    down[0] = descent
    for t in range(local_levels - 1, -1, -1):
        count = leaves // 2 ** (t + 1)
        values = [down[i] for i in range(count)]
        for i in range(count):
            spread = expand(values[i], both_t[table_base[t + 1] + i])
            node = node_base[t] + 2 * i
            down[2 * i] = far[node] + merge_gain * spread[:, :skel]
            down[2 * i + 1] = far[node + 1] + merge_gain * spread[:, skel:]

    def last(pair, carry):
        for k in range(2):
            leaf = 2 * pair + k
            part_ref[:, leaf_cols(leaf)] += merge_gain * expand(down[leaf], both_t[leaf])
        return carry

    lax.fori_loop(0, leaves // 2, last, 0)

    for copy in copies:
        copy.wait_send()

    def finish(sent, received):
        for copy in sent:
            copy.wait_send()
        for copy in received:
            copy.wait_recv()

    pl.when(dev > 0)(lambda: finish(halo(False), halo(True)))
    pl.when(dev < dev_count - 1)(lambda: finish(halo(True), halo(False)))


def near_kernel(
    leaves,
    leaf_rows,
    near_ref,
    count_ref,
    part_ref,
    p_hbm,
    w_hbm,
    halop_hbm,
    halow_hbm,
    out_ref,
    winp_ref,
    winw_ref,
    sem,
):
    copies = []
    for own, beside, window in ((p_hbm, halop_hbm, winp_ref), (w_hbm, halow_hbm, winw_ref)):
        for slot, src in ((1, own), (0, beside.at[0]), (2, beside.at[1])):
            copies.append(pltpu.make_async_copy(src, window.at[slot], sem.at[len(copies)]))
    for copy in copies:
        copy.start()
    for copy in copies:
        copy.wait()
    first_leaf = (lax.axis_index("dev") - 1) * leaves

    def one_leaf(leaf, carry):
        cols = pl.ds(pl.multiple_of(leaf * leaf_rows, leaf_rows), leaf_rows)
        out_ref[:, cols] = part_ref[:, cols]
        target = with_squares(winp_ref[1, :, cols], False)

        def one_slot(slot, inner):
            place = near_ref[slot, leaf] - first_leaf
            side = place // leaves
            other = pl.ds(pl.multiple_of((place - side * leaves) * leaf_rows, leaf_rows), leaf_rows)
            block = kernel_block(with_squares(winp_ref[side, :, other], True), target)
            out_ref[:, cols] += apply(winw_ref[side, :, other], block)
            return inner

        lax.fori_loop(1, count_ref[leaf], one_slot, 0)
        return carry

    lax.fori_loop(0, leaves, one_leaf, 0)


def per_device(
    dev_count, group_count, points, weights, near_leaves, near_count, leaf_perm, local_perm, upper_perm
):
    feat = points.shape[1]
    rhs = weights.shape[1]
    rows = points.shape[0]
    leaves, leaf_rows = leaf_perm.shape
    skel = leaf_rows // 2
    rounds = (dev_count * group_count).bit_length() - 1
    vmem = pl.BlockSpec(memory_space=pltpu.VMEM)
    smem = pl.BlockSpec(memory_space=pltpu.SMEM)
    hbm = pl.BlockSpec(memory_space=pltpu.HBM)
    part, win_p, win_w = pl.pallas_call(
        functools.partial(tree_kernel, leaves, leaf_rows, feat, dev_count, group_count),
        out_shape=[
            jax.ShapeDtypeStruct((rhs, rows), f32),
            jax.ShapeDtypeStruct((2, feat, rows), bf16),
            jax.ShapeDtypeStruct((2, rhs, rows), bf16),
        ],
        in_specs=[hbm] * 5,
        out_specs=[vmem, hbm, hbm],
        scratch_shapes=[
            pltpu.VMEM((leaves - 1 + rounds, 2, feat + rhs, skel), bf16),
            pltpu.VMEM((2 * leaves - 2 + rounds, leaf_rows, skel), bf16),
            pltpu.VMEM((2 * leaves - 2 + rounds, leaf_rows, skel), bf16),
            pltpu.VMEM((2 * leaves - 2 + rounds, rhs, skel), f32),
            pltpu.VMEM((leaves, rhs, skel), f32),
            pltpu.SemaphoreType.DMA((rounds,)),
            pltpu.SemaphoreType.DMA((rounds,)),
            pltpu.SemaphoreType.DMA((2, 2)),
            pltpu.SemaphoreType.DMA((2, 2)),
            pltpu.VMEM((feat, rows), bf16),
            pltpu.VMEM((rhs, rows), bf16),
            pltpu.VMEM(leaf_perm.shape, jnp.int32),
            pltpu.VMEM((leaves - 1, 1, leaf_rows), jnp.int32),
            pltpu.VMEM(upper_perm.shape, jnp.int32),
            pltpu.SemaphoreType.DMA((5,)),
        ],
        compiler_params=pltpu.CompilerParams(
            collective_id=0, has_side_effects=True, vmem_limit_bytes=62 * 2**20
        ),
        name="tree",
    )(points.T, weights.T, leaf_perm, jnp.transpose(local_perm, (1, 0, 2)), upper_perm)
    product = pl.pallas_call(
        functools.partial(near_kernel, leaves, leaf_rows),
        out_shape=jax.ShapeDtypeStruct((rhs, rows), f32),
        in_specs=[smem, smem, vmem, hbm, hbm, hbm, hbm],
        out_specs=vmem,
        scratch_shapes=[
            pltpu.VMEM((3, feat, rows), bf16),
            pltpu.VMEM((3, rhs, rows), bf16),
            pltpu.SemaphoreType.DMA((6,)),
        ],
        compiler_params=pltpu.CompilerParams(vmem_limit_bytes=62 * 2**20),
        name="near",
    )(near_leaves.T, near_count, part, points.T, weights.T, win_p, win_w)
    return product.T


def solution(mesh):
    sizes = dict(mesh.shape)
    both = ("group", "dev")
    in_specs = (
        P(both, None),
        P(both, None),
        P(both, None),
        P(both),
        P(both, None),
        P(both, None, None),
        P(),
    )
    return jax.shard_map(
        functools.partial(per_device, sizes["dev"], sizes["group"]),
        mesh=mesh,
        in_specs=in_specs,
        out_specs=P(both, None),
        check_vma=False,
    )
```

```python
import functools
import math

import jax
import jax.numpy as jnp
from jax import lax
from jax.experimental import pallas as pl
from jax.experimental.pallas import tpu as pltpu
from jax.sharding import PartitionSpec as P

spread_width = 10.0
merge_gain = 0.8408964152537145
exp2_scale = 2.0 / spread_width * math.log2(math.e)
bf16 = jnp.bfloat16
f32 = jnp.float32


def half_squares(coords):
    wide = coords.astype(f32)
    total = -0.5 * jnp.sum(wide * wide, axis=0, keepdims=True)
    high = total.astype(bf16).astype(f32)
    rest = total - high
    mid = rest.astype(bf16).astype(f32)
    return high, mid, rest - mid


def with_squares(coords, squares_first):
    high, mid, low = half_squares(coords)
    shape = (16, coords.shape[1])
    row = lax.broadcasted_iota(jnp.int32, shape, 0)
    at = 0 if squares_first else 3
    ones = (row >= 3 - at) & (row < 6 - at)
    extra = jnp.where(ones, 1.0, 0.0)
    for offset, part in enumerate((high, mid, low)):
        extra = jnp.where(row == at + offset, jnp.broadcast_to(part, shape), extra)
    return jnp.concatenate([coords, extra.astype(bf16)], axis=0)


def kernel_block(source, target):
    inner = lax.dot_general(source, target, (((0,), (0,)), ((), ())), preferred_element_type=f32)
    return jnp.exp2(inner * exp2_scale).astype(bf16)


def apply(rhs, block):
    return jnp.dot(rhs, block, preferred_element_type=f32)


def apply_flipped(rhs, block):
    return lax.dot_general(rhs, block, (((1,), (1,)), ((), ())), preferred_element_type=f32)


def tables(order, head_ref, both_ref, at):
    size = order.shape[1]
    half = size // 2
    row = lax.broadcasted_iota(jnp.int32, (size, half), 0)
    head = order[:, :half] == row
    tail = order[:, half:] == row
    head_ref[at] = jnp.where(head, 1.0, 0.0).astype(bf16)
    both_ref[at] = jnp.where(head | tail, 1.0, 0.0).astype(bf16)


def merge(coords, rhs, head, both):
    picked = jnp.dot(coords, head, preferred_element_type=f32).astype(bf16)
    summed = merge_gain * jnp.dot(rhs, both, preferred_element_type=f32)
    return jnp.concatenate([picked, summed.astype(bf16)], axis=0)


def expand(values, both):
    high = values.astype(bf16)
    low = (values - high.astype(f32)).astype(bf16)
    spread = apply_flipped(jnp.concatenate([high, low], axis=0), both)
    rows = values.shape[0]
    return spread[:rows] + spread[rows:]


def tree_kernel(
    leaves,
    leaf_rows,
    feat,
    dev_count,
    group_count,
    p_hbm,
    w_hbm,
    leaf_hbm,
    local_hbm,
    upper_hbm,
    part_ref,
    winp_ref,
    winw_ref,
    stack,
    head_t,
    both_t,
    far,
    down,
    send_sem,
    recv_sem,
    halo_send,
    halo_recv,
    p_ref,
    w_ref,
    leaf_ref,
    local_ref,
    upper_ref,
    load_sem,
    relay,
    relay_sem,
):
    skel = leaf_rows // 2
    devices = dev_count * group_count
    dev_bits = dev_count.bit_length() - 1
    group_bits = group_count.bit_length() - 1
    rounds = dev_bits + group_bits
    local_levels = leaves.bit_length() - 1
    dev = lax.axis_index("dev")
    group = lax.axis_index("group")
    flat = group * dev_count + dev

    def partner(height):
        if height < dev_bits:
            side = dev // 2**height % 2
            return {"dev": dev + (1 - 2 * side) * 2**height}, side
        stride = 2 ** (height - dev_bits)
        side = group // stride % 2
        return {"group": group + (1 - 2 * side) * stride}, side

    loads = [
        pltpu.make_async_copy(src, dst, load_sem.at[k])
        for k, (src, dst) in enumerate(
            (
                (leaf_hbm, leaf_ref),
                (p_hbm, p_ref),
                (w_hbm, w_ref),
                (local_hbm, local_ref),
                (upper_hbm, upper_ref),
            )
        )
    ]
    for load in loads:
        load.start()
    barrier = pltpu.get_barrier_semaphore()
    for height in range(rounds):
        pl.semaphore_signal(
            barrier, inc=1, device_id=partner(height)[0], device_id_type=pl.DeviceIdType.MESH
        )

    beside = dev + 2 * lax.rem(dev, 2) - 1
    has_beside = (beside >= 0) & (beside < dev_count)

    @pl.when(has_beside)
    def _():
        pl.semaphore_signal(
            barrier, inc=1, device_id={"dev": beside}, device_id_type=pl.DeviceIdType.MESH
        )

    greeted = rounds + has_beside.astype(jnp.int32)
    relayed = dev_count == 8
    if relayed:
        across = jnp.where(dev < 4, 3 - dev, 11 - dev)
        has_across = (dev == 0) | (dev == 3) | (dev == 4) | (dev == 7)

        @pl.when(has_across)
        def _():
            pl.semaphore_signal(
                barrier, inc=1, device_id={"dev": across}, device_id_type=pl.DeviceIdType.MESH
            )

        greeted = greeted + has_across.astype(jnp.int32)
    pl.semaphore_wait(barrier, greeted)

    def halo(to_right):
        other = lax.rem(dev + 1, dev_count) if to_right else lax.rem(dev + dev_count - 1, dev_count)
        slot = 0 if to_right else 1
        row = 1 if to_right else 0
        return [
            pltpu.make_async_remote_copy(
                src_ref=src,
                dst_ref=dst.at[slot],
                send_sem=halo_send.at[row, k],
                recv_sem=halo_recv.at[row, k],
                device_id={"dev": other},
                device_id_type=pl.DeviceIdType.MESH,
            )
            for k, (src, dst) in enumerate(((p_hbm, winp_ref), (w_hbm, winw_ref)))
        ]

    def start(copies):
        for copy in copies:
            copy.start()

    def first_leg(to_right):
        row = 1 if to_right else 0
        return pltpu.make_async_remote_copy(
            src_ref=p_hbm,
            dst_ref=relay,
            send_sem=halo_send.at[row, 0],
            recv_sem=relay_sem.at[0],
            device_id={"dev": 7 if to_right else 0},
            device_id_type=pl.DeviceIdType.MESH,
        )

    def second_leg(to_right):
        slot, row, target = (0, 1, 4) if to_right else (1, 0, 3)
        return pltpu.make_async_remote_copy(
            src_ref=relay,
            dst_ref=winp_ref.at[slot],
            send_sem=relay_sem.at[1],
            recv_sem=halo_recv.at[row, 0],
            device_id={"dev": target},
            device_id_type=pl.DeviceIdType.MESH,
        )

    def forward(to_right):
        first_leg(to_right).wait_recv()
        second_leg(to_right).start()

    if relayed:
        pl.when((dev > 0) & (dev != 4))(lambda: start(halo(False)[:1]))
        pl.when((dev < dev_count - 1) & (dev != 3))(lambda: start(halo(True)[:1]))
        pl.when(dev == 3)(lambda: first_leg(True).start())
        pl.when(dev == 4)(lambda: first_leg(False).start())
    else:
        pl.when(dev > 0)(lambda: start(halo(False)[:1]))
        pl.when(dev < dev_count - 1)(lambda: start(halo(True)[:1]))
    for load in loads:
        load.wait()

    def leaf_cols(leaf):
        return pl.ds(pl.multiple_of(leaf * leaf_rows, leaf_rows), leaf_rows)

    pair_base = [leaves - leaves // 2**t for t in range(local_levels)]
    top_pair = leaves - 1
    node_base = [2 * base for base in pair_base]
    top_node = 2 * top_pair
    table_base = [0] + [leaves + base for base in pair_base]
    top_table = 2 * leaves - 1

    def up_leaves(pair, carry):
        for k in range(2):
            leaf = 2 * pair + k
            tables(leaf_ref[pl.ds(leaf, 1), :], head_t, both_t, leaf)
            cols = leaf_cols(leaf)
            stack[pair, k] = merge(p_ref[:, cols], w_ref[:, cols], head_t[leaf], both_t[leaf])
        return carry

    lax.fori_loop(0, leaves // 2, up_leaves, 0)

    def merge_pair(pair, table):
        two = jnp.concatenate([stack[pair, 0], stack[pair, 1]], axis=1)
        return merge(two[:feat], two[feat:], head_t[table], both_t[table])

    side0 = partner(0)[1]
    for t in range(local_levels):
        count = leaves // 2 ** (t + 1)
        for i in range(count):
            row = pair_base[t] + i
            tables(local_ref[row], head_t, both_t, table_base[t + 1] + i)
            merged = merge_pair(pair_base[t] + i, table_base[t + 1] + i)
            if t + 1 < local_levels:
                stack[pair_base[t + 1] + i // 2, i % 2] = merged
            else:
                stack[top_pair, side0] = merged

    def local_far(pair, carry):
        first, second = stack[pair, 0], stack[pair, 1]
        block = kernel_block(with_squares(first[:feat], True), with_squares(second[:feat], False))
        far[2 * pair + 1] = apply(first[feat:], block)
        far[2 * pair] = apply_flipped(second[feat:], block)
        return carry

    def near_own(leaf, carry):
        cols = leaf_cols(leaf)
        coords = p_ref[:, cols]
        block = kernel_block(with_squares(coords, True), with_squares(coords, False))
        part_ref[:, cols] = apply(w_ref[:, cols], block)
        return carry

    def cross_far(height):
        side = partner(height)[1]
        own = stack[top_pair + height, side]
        other = stack[top_pair + height, 1 - side]
        block = kernel_block(with_squares(other[:feat], True), with_squares(own[:feat], False))
        far[top_node + height] = apply(other[feat:], block)

    def exchange(height):
        target, side = partner(height)
        return pltpu.make_async_remote_copy(
            src_ref=stack.at[top_pair + height, side],
            dst_ref=stack.at[top_pair + height, side],
            send_sem=send_sem.at[height],
            recv_sem=recv_sem.at[height],
            device_id=target,
            device_id_type=pl.DeviceIdType.MESH,
        )

    shares = max(rounds - 1, 1)
    bounds = [leaves * k // shares for k in range(shares + 1)]
    far_bounds = [(leaves - 1) * k // shares for k in range(shares + 1)]
    copies = []
    for height in range(rounds):
        copy = exchange(height)
        copy.start()
        copies.append(copy)
        if height == 0:
            for level in range(rounds - 1):
                row = devices - devices // 2**level + flat // 2 ** (level + 1)
                tables(upper_ref[pl.ds(row, 1), :], head_t, both_t, top_table + level)
        else:
            cross_far(height - 1)
            if bounds[height] > bounds[height - 1]:
                lax.fori_loop(bounds[height - 1], bounds[height], near_own, 0)
            if far_bounds[height] > far_bounds[height - 1]:
                lax.fori_loop(far_bounds[height - 1], far_bounds[height], local_far, 0)
        copy.wait_recv()
        if height == min(1, rounds - 1):
            pl.when(dev > 0)(lambda: start(halo(False)[1:]))
            pl.when(dev < dev_count - 1)(lambda: start(halo(True)[1:]))
            if relayed:
                pl.when(dev == 7)(lambda: forward(True))
                pl.when(dev == 0)(lambda: forward(False))
        if height + 1 < rounds:
            stack[top_pair + height + 1, partner(height + 1)[1]] = merge_pair(
                top_pair + height, top_table + height
            )
    cross_far(rounds - 1)
    if rounds == 1:
        lax.fori_loop(0, leaves, near_own, 0)
        lax.fori_loop(0, leaves - 1, local_far, 0)

    descent = far[top_node + rounds - 1]
    for height in range(rounds - 2, -1, -1):
        rows = pl.ds(pl.multiple_of(partner(height + 0)[1] * skel, skel), skel)
        spread = expand(descent, both_t[top_table + height, rows, :])
        descent = far[top_node + height] + merge_gain * spread
    down[0] = descent
    for t in range(local_levels - 1, -1, -1):
        count = leaves // 2 ** (t + 1)
        values = [down[i] for i in range(count)]
        for i in range(count):
            spread = expand(values[i], both_t[table_base[t + 1] + i])
            node = node_base[t] + 2 * i
            down[2 * i] = far[node] + merge_gain * spread[:, :skel]
            down[2 * i + 1] = far[node + 1] + merge_gain * spread[:, skel:]

    def last(pair, carry):
        for k in range(2):
            leaf = 2 * pair + k
            part_ref[:, leaf_cols(leaf)] += merge_gain * expand(down[leaf], both_t[leaf])
        return carry

    lax.fori_loop(0, leaves // 2, last, 0)

    for copy in copies:
        copy.wait_send()
    if relayed:
        pl.when(dev == 7)(lambda: second_leg(True).wait_send())
        pl.when(dev == 0)(lambda: second_leg(False).wait_send())

    def finish(sent, received):
        for copy in sent:
            copy.wait_send()
        for copy in received:
            copy.wait_recv()

    pl.when(dev > 0)(lambda: finish(halo(False), halo(True)))
    pl.when(dev < dev_count - 1)(lambda: finish(halo(True), halo(False)))


def near_kernel(
    leaves,
    leaf_rows,
    near_ref,
    count_ref,
    part_ref,
    p_hbm,
    w_hbm,
    halop_hbm,
    halow_hbm,
    out_ref,
    winp_ref,
    winw_ref,
    sem,
):
    copies = []
    for own, beside, window in ((p_hbm, halop_hbm, winp_ref), (w_hbm, halow_hbm, winw_ref)):
        for slot, src in ((1, own), (0, beside.at[0]), (2, beside.at[1])):
            copies.append(pltpu.make_async_copy(src, window.at[slot], sem.at[len(copies)]))
    for copy in copies:
        copy.start()
    for copy in copies:
        copy.wait()
    first_leaf = (lax.axis_index("dev") - 1) * leaves

    def one_leaf(leaf, carry):
        cols = pl.ds(pl.multiple_of(leaf * leaf_rows, leaf_rows), leaf_rows)
        out_ref[:, cols] = part_ref[:, cols]
        target = with_squares(winp_ref[1, :, cols], False)

        def one_slot(slot, inner):
            place = near_ref[slot, leaf] - first_leaf
            side = place // leaves
            other = pl.ds(pl.multiple_of((place - side * leaves) * leaf_rows, leaf_rows), leaf_rows)
            block = kernel_block(with_squares(winp_ref[side, :, other], True), target)
            out_ref[:, cols] += apply(winw_ref[side, :, other], block)
            return inner

        lax.fori_loop(1, count_ref[leaf], one_slot, 0)
        return carry

    lax.fori_loop(0, leaves, one_leaf, 0)


def per_device(
    dev_count, group_count, points, weights, near_leaves, near_count, leaf_perm, local_perm, upper_perm
):
    feat = points.shape[1]
    rhs = weights.shape[1]
    rows = points.shape[0]
    leaves, leaf_rows = leaf_perm.shape
    skel = leaf_rows // 2
    rounds = (dev_count * group_count).bit_length() - 1
    vmem = pl.BlockSpec(memory_space=pltpu.VMEM)
    smem = pl.BlockSpec(memory_space=pltpu.SMEM)
    hbm = pl.BlockSpec(memory_space=pltpu.HBM)
    part, win_p, win_w = pl.pallas_call(
        functools.partial(tree_kernel, leaves, leaf_rows, feat, dev_count, group_count),
        out_shape=[
            jax.ShapeDtypeStruct((rhs, rows), f32),
            jax.ShapeDtypeStruct((2, feat, rows), bf16),
            jax.ShapeDtypeStruct((2, rhs, rows), bf16),
        ],
        in_specs=[hbm] * 5,
        out_specs=[vmem, hbm, hbm],
        scratch_shapes=[
            pltpu.VMEM((leaves - 1 + rounds, 2, feat + rhs, skel), bf16),
            pltpu.VMEM((2 * leaves - 2 + rounds, leaf_rows, skel), bf16),
            pltpu.VMEM((2 * leaves - 2 + rounds, leaf_rows, skel), bf16),
            pltpu.VMEM((2 * leaves - 2 + rounds, rhs, skel), f32),
            pltpu.VMEM((leaves, rhs, skel), f32),
            pltpu.SemaphoreType.DMA((rounds,)),
            pltpu.SemaphoreType.DMA((rounds,)),
            pltpu.SemaphoreType.DMA((2, 2)),
            pltpu.SemaphoreType.DMA((2, 2)),
            pltpu.VMEM((feat, rows), bf16),
            pltpu.VMEM((rhs, rows), bf16),
            pltpu.VMEM(leaf_perm.shape, jnp.int32),
            pltpu.VMEM((leaves - 1, 1, leaf_rows), jnp.int32),
            pltpu.VMEM(upper_perm.shape, jnp.int32),
            pltpu.SemaphoreType.DMA((5,)),
            pltpu.VMEM((feat, rows), bf16),
            pltpu.SemaphoreType.DMA((2,)),
        ],
        compiler_params=pltpu.CompilerParams(
            collective_id=0, has_side_effects=True, vmem_limit_bytes=62 * 2**20
        ),
        name="tree",
    )(points.T, weights.T, leaf_perm, jnp.transpose(local_perm, (1, 0, 2)), upper_perm)
    product = pl.pallas_call(
        functools.partial(near_kernel, leaves, leaf_rows),
        out_shape=jax.ShapeDtypeStruct((rhs, rows), f32),
        in_specs=[smem, smem, vmem, hbm, hbm, hbm, hbm],
        out_specs=vmem,
        scratch_shapes=[
            pltpu.VMEM((3, feat, rows), bf16),
            pltpu.VMEM((3, rhs, rows), bf16),
            pltpu.SemaphoreType.DMA((6,)),
        ],
        compiler_params=pltpu.CompilerParams(vmem_limit_bytes=62 * 2**20),
        name="near",
    )(near_leaves.T, near_count, part, points.T, weights.T, win_p, win_w)
    return product.T


def solution(mesh):
    sizes = dict(mesh.shape)
    both = ("group", "dev")
    in_specs = (
        P(both, None),
        P(both, None),
        P(both, None),
        P(both),
        P(both, None),
        P(both, None, None),
        P(),
    )
    return jax.shard_map(
        functools.partial(per_device, sizes["dev"], sizes["group"]),
        mesh=mesh,
        in_specs=in_specs,
        out_specs=P(both, None),
        check_vma=False,
    )
```

```python
import functools
import math

import jax
import jax.numpy as jnp
from jax import lax
from jax.experimental import pallas as pl
from jax.experimental.pallas import tpu as pltpu
from jax.sharding import PartitionSpec as P

spread_width = 10.0
merge_gain = 0.8408964152537145
exp2_scale = 2.0 / spread_width * math.log2(math.e)
bf16 = jnp.bfloat16
f32 = jnp.float32


def half_squares(coords):
    wide = coords.astype(f32)
    total = -0.5 * jnp.sum(wide * wide, axis=0, keepdims=True)
    high = total.astype(bf16).astype(f32)
    rest = total - high
    mid = rest.astype(bf16).astype(f32)
    return high, mid, rest - mid


def with_squares(coords, squares_first):
    high, mid, low = half_squares(coords)
    shape = (16, coords.shape[1])
    row = lax.broadcasted_iota(jnp.int32, shape, 0)
    at = 0 if squares_first else 3
    ones = (row >= 3 - at) & (row < 6 - at)
    extra = jnp.where(ones, 1.0, 0.0)
    for offset, part in enumerate((high, mid, low)):
        extra = jnp.where(row == at + offset, jnp.broadcast_to(part, shape), extra)
    return jnp.concatenate([coords, extra.astype(bf16)], axis=0)


def kernel_block(source, target):
    inner = lax.dot_general(source, target, (((0,), (0,)), ((), ())), preferred_element_type=f32)
    return jnp.exp2(inner * exp2_scale).astype(bf16)


def apply(rhs, block):
    return jnp.dot(rhs, block, preferred_element_type=f32)


def apply_flipped(rhs, block):
    return lax.dot_general(rhs, block, (((1,), (1,)), ((), ())), preferred_element_type=f32)


def tables(order, head_ref, both_ref, at):
    size = order.shape[1]
    half = size // 2
    row = lax.broadcasted_iota(jnp.int32, (size, half), 0)
    head = order[:, :half] == row
    tail = order[:, half:] == row
    head_ref[at] = jnp.where(head, 1.0, 0.0).astype(bf16)
    both_ref[at] = jnp.where(head | tail, 1.0, 0.0).astype(bf16)


def merge(coords, rhs, head, both):
    picked = jnp.dot(coords, head, preferred_element_type=f32).astype(bf16)
    summed = merge_gain * jnp.dot(rhs, both, preferred_element_type=f32)
    return jnp.concatenate([picked, summed.astype(bf16)], axis=0)


def expand(values, both):
    high = values.astype(bf16)
    low = (values - high.astype(f32)).astype(bf16)
    spread = apply_flipped(jnp.concatenate([high, low], axis=0), both)
    rows = values.shape[0]
    return spread[:rows] + spread[rows:]


def tree_kernel(
    leaves,
    leaf_rows,
    feat,
    dev_count,
    group_count,
    p_hbm,
    w_hbm,
    leaf_hbm,
    local_hbm,
    upper_hbm,
    part_ref,
    winp_ref,
    winw_ref,
    stack,
    head_t,
    both_t,
    far,
    down,
    send_sem,
    recv_sem,
    halo_send,
    halo_recv,
    p_ref,
    w_ref,
    leaf_ref,
    local_ref,
    upper_ref,
    load_sem,
    relay,
    relay_sem,
):
    skel = leaf_rows // 2
    devices = dev_count * group_count
    dev_bits = dev_count.bit_length() - 1
    group_bits = group_count.bit_length() - 1
    rounds = dev_bits + group_bits
    local_levels = leaves.bit_length() - 1
    dev = lax.axis_index("dev")
    group = lax.axis_index("group")
    flat = group * dev_count + dev

    def partner(height):
        if height < dev_bits:
            side = dev // 2**height % 2
            return {"dev": dev + (1 - 2 * side) * 2**height}, side
        stride = 2 ** (height - dev_bits)
        side = group // stride % 2
        return {"group": group + (1 - 2 * side) * stride}, side

    loads = [
        pltpu.make_async_copy(src, dst, load_sem.at[k])
        for k, (src, dst) in enumerate(
            (
                (leaf_hbm, leaf_ref),
                (p_hbm, p_ref),
                (w_hbm, w_ref),
                (local_hbm, local_ref),
                (upper_hbm, upper_ref),
            )
        )
    ]
    for load in loads:
        load.start()
    barrier = pltpu.get_barrier_semaphore()
    for height in range(rounds):
        pl.semaphore_signal(
            barrier, inc=1, device_id=partner(height)[0], device_id_type=pl.DeviceIdType.MESH
        )

    beside = dev + 2 * lax.rem(dev, 2) - 1
    has_beside = (beside >= 0) & (beside < dev_count)

    @pl.when(has_beside)
    def _():
        pl.semaphore_signal(
            barrier, inc=1, device_id={"dev": beside}, device_id_type=pl.DeviceIdType.MESH
        )

    greeted = rounds + has_beside.astype(jnp.int32)
    relayed = dev_count == 8
    if relayed:
        across = jnp.where(dev < 4, 3 - dev, 11 - dev)
        has_across = (dev == 0) | (dev == 3) | (dev == 4) | (dev == 7)

        @pl.when(has_across)
        def _():
            pl.semaphore_signal(
                barrier, inc=1, device_id={"dev": across}, device_id_type=pl.DeviceIdType.MESH
            )

        greeted = greeted + has_across.astype(jnp.int32)
    pl.semaphore_wait(barrier, greeted)

    def halo(to_right):
        other = lax.rem(dev + 1, dev_count) if to_right else lax.rem(dev + dev_count - 1, dev_count)
        slot = 0 if to_right else 1
        row = 1 if to_right else 0
        return [
            pltpu.make_async_remote_copy(
                src_ref=src,
                dst_ref=dst.at[slot],
                send_sem=halo_send.at[row, k],
                recv_sem=halo_recv.at[row, k],
                device_id={"dev": other},
                device_id_type=pl.DeviceIdType.MESH,
            )
            for k, (src, dst) in enumerate(((p_hbm, winp_ref), (w_hbm, winw_ref)))
        ]

    def start(copies):
        for copy in copies:
            copy.start()

    def first_leg(to_right):
        row = 1 if to_right else 0
        return pltpu.make_async_remote_copy(
            src_ref=p_hbm,
            dst_ref=relay,
            send_sem=halo_send.at[row, 0],
            recv_sem=relay_sem.at[0],
            device_id={"dev": 7 if to_right else 0},
            device_id_type=pl.DeviceIdType.MESH,
        )

    def second_leg(to_right):
        slot, row, target = (0, 1, 4) if to_right else (1, 0, 3)
        return pltpu.make_async_remote_copy(
            src_ref=relay,
            dst_ref=winp_ref.at[slot],
            send_sem=relay_sem.at[1],
            recv_sem=halo_recv.at[row, 0],
            device_id={"dev": target},
            device_id_type=pl.DeviceIdType.MESH,
        )

    def forward(to_right):
        first_leg(to_right).wait_recv()
        second_leg(to_right).start()

    if relayed:
        pl.when((dev > 0) & (dev != 4))(lambda: start(halo(False)[:1]))
        pl.when((dev < dev_count - 1) & (dev != 3))(lambda: start(halo(True)[:1]))
        pl.when(dev == 3)(lambda: first_leg(True).start())
        pl.when(dev == 4)(lambda: first_leg(False).start())
    else:
        pl.when(dev > 0)(lambda: start(halo(False)[:1]))
        pl.when(dev < dev_count - 1)(lambda: start(halo(True)[:1]))
    for load in loads:
        load.wait()

    def leaf_cols(leaf):
        return pl.ds(pl.multiple_of(leaf * leaf_rows, leaf_rows), leaf_rows)

    pair_base = [leaves - leaves // 2**t for t in range(local_levels)]
    top_pair = leaves - 1
    node_base = [2 * base for base in pair_base]
    top_node = 2 * top_pair
    table_base = [0] + [leaves + base for base in pair_base]
    top_table = 2 * leaves - 1

    def up_leaves(pair, carry):
        for k in range(2):
            leaf = 2 * pair + k
            tables(leaf_ref[pl.ds(leaf, 1), :], head_t, both_t, leaf)
            cols = leaf_cols(leaf)
            stack[pair, k] = merge(p_ref[:, cols], w_ref[:, cols], head_t[leaf], both_t[leaf])
        return carry

    lax.fori_loop(0, leaves // 2, up_leaves, 0)

    def merge_pair(pair, table):
        two = jnp.concatenate([stack[pair, 0], stack[pair, 1]], axis=1)
        return merge(two[:feat], two[feat:], head_t[table], both_t[table])

    side0 = partner(0)[1]
    for t in range(local_levels):
        count = leaves // 2 ** (t + 1)
        for i in range(count):
            row = pair_base[t] + i
            tables(local_ref[row], head_t, both_t, table_base[t + 1] + i)
            merged = merge_pair(pair_base[t] + i, table_base[t + 1] + i)
            if t + 1 < local_levels:
                stack[pair_base[t + 1] + i // 2, i % 2] = merged
            else:
                stack[top_pair, side0] = merged

    def local_far(pair, carry):
        first, second = stack[pair, 0], stack[pair, 1]
        block = kernel_block(with_squares(first[:feat], True), with_squares(second[:feat], False))
        far[2 * pair + 1] = apply(first[feat:], block)
        far[2 * pair] = apply_flipped(second[feat:], block)
        return carry

    def near_own(leaf, carry):
        cols = leaf_cols(leaf)
        coords = p_ref[:, cols]
        block = kernel_block(with_squares(coords, True), with_squares(coords, False))
        part_ref[:, cols] = apply(w_ref[:, cols], block)
        return carry

    def cross_far(height):
        side = partner(height)[1]
        own = stack[top_pair + height, side]
        other = stack[top_pair + height, 1 - side]
        block = kernel_block(with_squares(other[:feat], True), with_squares(own[:feat], False))
        far[top_node + height] = apply(other[feat:], block)

    def exchange(height):
        target, side = partner(height)
        return pltpu.make_async_remote_copy(
            src_ref=stack.at[top_pair + height, side],
            dst_ref=stack.at[top_pair + height, side],
            send_sem=send_sem.at[height],
            recv_sem=recv_sem.at[height],
            device_id=target,
            device_id_type=pl.DeviceIdType.MESH,
        )

    shares = max(rounds - 1, 1)
    bounds = [leaves * k // shares for k in range(shares + 1)]
    far_bounds = [(leaves - 1) * k // shares for k in range(shares + 1)]
    copies = []
    for height in range(rounds):
        copy = exchange(height)
        copy.start()
        copies.append(copy)
        if height == 0:
            for level in range(rounds - 1):
                row = devices - devices // 2**level + flat // 2 ** (level + 1)
                tables(upper_ref[pl.ds(row, 1), :], head_t, both_t, top_table + level)
        else:
            cross_far(height - 1)
            if bounds[height] > bounds[height - 1]:
                lax.fori_loop(bounds[height - 1], bounds[height], near_own, 0)
            if far_bounds[height] > far_bounds[height - 1]:
                lax.fori_loop(far_bounds[height - 1], far_bounds[height], local_far, 0)
        copy.wait_recv()
        if height == 0:
            pl.when(dev > 0)(lambda: start(halo(False)[1:]))
            pl.when(dev < dev_count - 1)(lambda: start(halo(True)[1:]))
        if height == 1 and relayed:
            pl.when(dev == 7)(lambda: forward(True))
            pl.when(dev == 0)(lambda: forward(False))
        if height + 1 < rounds:
            stack[top_pair + height + 1, partner(height + 1)[1]] = merge_pair(
                top_pair + height, top_table + height
            )
    cross_far(rounds - 1)
    if rounds == 1:
        lax.fori_loop(0, leaves, near_own, 0)
        lax.fori_loop(0, leaves - 1, local_far, 0)

    descent = far[top_node + rounds - 1]
    for height in range(rounds - 2, -1, -1):
        rows = pl.ds(pl.multiple_of(partner(height + 0)[1] * skel, skel), skel)
        spread = expand(descent, both_t[top_table + height, rows, :])
        descent = far[top_node + height] + merge_gain * spread
    down[0] = descent
    for t in range(local_levels - 1, -1, -1):
        count = leaves // 2 ** (t + 1)
        values = [down[i] for i in range(count)]
        for i in range(count):
            spread = expand(values[i], both_t[table_base[t + 1] + i])
            node = node_base[t] + 2 * i
            down[2 * i] = far[node] + merge_gain * spread[:, :skel]
            down[2 * i + 1] = far[node + 1] + merge_gain * spread[:, skel:]

    def last(pair, carry):
        for k in range(2):
            leaf = 2 * pair + k
            part_ref[:, leaf_cols(leaf)] += merge_gain * expand(down[leaf], both_t[leaf])
        return carry

    lax.fori_loop(0, leaves // 2, last, 0)

    for copy in copies:
        copy.wait_send()
    if relayed:
        pl.when(dev == 7)(lambda: second_leg(True).wait_send())
        pl.when(dev == 0)(lambda: second_leg(False).wait_send())

    def finish(sent, received):
        for copy in sent:
            copy.wait_send()
        for copy in received:
            copy.wait_recv()

    pl.when(dev > 0)(lambda: finish(halo(False), halo(True)))
    pl.when(dev < dev_count - 1)(lambda: finish(halo(True), halo(False)))


def near_kernel(
    leaves,
    leaf_rows,
    near_ref,
    count_ref,
    part_ref,
    p_hbm,
    w_hbm,
    halop_hbm,
    halow_hbm,
    out_ref,
    winp_ref,
    winw_ref,
    sem,
):
    copies = []
    for own, beside, window in ((p_hbm, halop_hbm, winp_ref), (w_hbm, halow_hbm, winw_ref)):
        for slot, src in ((1, own), (0, beside.at[0]), (2, beside.at[1])):
            copies.append(pltpu.make_async_copy(src, window.at[slot], sem.at[len(copies)]))
    for copy in copies:
        copy.start()
    for copy in copies:
        copy.wait()
    first_leaf = (lax.axis_index("dev") - 1) * leaves

    def one_leaf(leaf, carry):
        cols = pl.ds(pl.multiple_of(leaf * leaf_rows, leaf_rows), leaf_rows)
        out_ref[:, cols] = part_ref[:, cols]
        target = with_squares(winp_ref[1, :, cols], False)

        def one_slot(slot, inner):
            place = near_ref[slot, leaf] - first_leaf
            side = place // leaves
            other = pl.ds(pl.multiple_of((place - side * leaves) * leaf_rows, leaf_rows), leaf_rows)
            block = kernel_block(with_squares(winp_ref[side, :, other], True), target)
            out_ref[:, cols] += apply(winw_ref[side, :, other], block)
            return inner

        lax.fori_loop(1, count_ref[leaf], one_slot, 0)
        return carry

    lax.fori_loop(0, leaves, one_leaf, 0)


def per_device(
    dev_count, group_count, points, weights, near_leaves, near_count, leaf_perm, local_perm, upper_perm
):
    feat = points.shape[1]
    rhs = weights.shape[1]
    rows = points.shape[0]
    leaves, leaf_rows = leaf_perm.shape
    skel = leaf_rows // 2
    rounds = (dev_count * group_count).bit_length() - 1
    vmem = pl.BlockSpec(memory_space=pltpu.VMEM)
    smem = pl.BlockSpec(memory_space=pltpu.SMEM)
    hbm = pl.BlockSpec(memory_space=pltpu.HBM)
    part, win_p, win_w = pl.pallas_call(
        functools.partial(tree_kernel, leaves, leaf_rows, feat, dev_count, group_count),
        out_shape=[
            jax.ShapeDtypeStruct((rhs, rows), f32),
            jax.ShapeDtypeStruct((2, feat, rows), bf16),
            jax.ShapeDtypeStruct((2, rhs, rows), bf16),
        ],
        in_specs=[hbm] * 5,
        out_specs=[vmem, hbm, hbm],
        scratch_shapes=[
            pltpu.VMEM((leaves - 1 + rounds, 2, feat + rhs, skel), bf16),
            pltpu.VMEM((2 * leaves - 2 + rounds, leaf_rows, skel), bf16),
            pltpu.VMEM((2 * leaves - 2 + rounds, leaf_rows, skel), bf16),
            pltpu.VMEM((2 * leaves - 2 + rounds, rhs, skel), f32),
            pltpu.VMEM((leaves, rhs, skel), f32),
            pltpu.SemaphoreType.DMA((rounds,)),
            pltpu.SemaphoreType.DMA((rounds,)),
            pltpu.SemaphoreType.DMA((2, 2)),
            pltpu.SemaphoreType.DMA((2, 2)),
            pltpu.VMEM((feat, rows), bf16),
            pltpu.VMEM((rhs, rows), bf16),
            pltpu.VMEM(leaf_perm.shape, jnp.int32),
            pltpu.VMEM((leaves - 1, 1, leaf_rows), jnp.int32),
            pltpu.VMEM(upper_perm.shape, jnp.int32),
            pltpu.SemaphoreType.DMA((5,)),
            pltpu.VMEM((feat, rows), bf16),
            pltpu.SemaphoreType.DMA((2,)),
        ],
        compiler_params=pltpu.CompilerParams(
            collective_id=0, has_side_effects=True, vmem_limit_bytes=62 * 2**20
        ),
        name="tree",
    )(points.T, weights.T, leaf_perm, jnp.transpose(local_perm, (1, 0, 2)), upper_perm)
    product = pl.pallas_call(
        functools.partial(near_kernel, leaves, leaf_rows),
        out_shape=jax.ShapeDtypeStruct((rhs, rows), f32),
        in_specs=[smem, smem, vmem, hbm, hbm, hbm, hbm],
        out_specs=vmem,
        scratch_shapes=[
            pltpu.VMEM((3, feat, rows), bf16),
            pltpu.VMEM((3, rhs, rows), bf16),
            pltpu.SemaphoreType.DMA((6,)),
        ],
        compiler_params=pltpu.CompilerParams(vmem_limit_bytes=62 * 2**20),
        name="near",
    )(near_leaves.T, near_count, part, points.T, weights.T, win_p, win_w)
    return product.T


def solution(mesh):
    sizes = dict(mesh.shape)
    both = ("group", "dev")
    in_specs = (
        P(both, None),
        P(both, None),
        P(both, None),
        P(both),
        P(both, None),
        P(both, None, None),
        P(),
    )
    return jax.shard_map(
        functools.partial(per_device, sizes["dev"], sizes["group"]),
        mesh=mesh,
        in_specs=in_specs,
        out_specs=P(both, None),
        check_vma=False,
    )
```
